128 devices in a mesh: ctx: 16 (over y_lo, z, core), head: 8 (over y_hi, x).
Axes of the slice: x: 4, y: 4 (y_hi: 2, y_lo: 2; y = y_hi * 2 + y_lo), z: 4, core: 2. Of those that a mesh axis runs over, the one named last changes fastest.
Arguments:
- queries: bfloat16 [16384, 8192], P(('ctx', 'head')), may hold values from -128 to 128
- keys: bfloat16 [16384, 1024], P(('ctx', 'head')), may hold values from -8 to 8
- values: bfloat16 [16384, 1024], P(('ctx', 'head')), may hold values from -6 to 6
- doc_lengths: int32 [8], replicated, may hold values from 1 to 6144, 16384 in all
Outputs:
- attended: bfloat16 [16384, 8192], P(('ctx', 'head'))
The draws below stay inside these ranges and needn't reach their ends.
Inputs may be any that keep to these rules, and one draw needn't show every extreme that they name: `doc_lengths`: each document has 1 to 6144 tokens, the longest exactly 6144; they sum to 16384.
All inputs are finite; a program needn't handle non-finite values.
Results may differ from the reference program's by a relative error of at most 0.005.
Values may be sent and summed in bfloat16 or wider, within the bound.
A program may use at most 128 MiB of HBM per device.

```python
import math
import jax
import jax.numpy as jnp
import numpy as np
from jax import lax

HEADS = 64
KV_HEADS = 8
HEAD_DIM = 128
NDOCS = 8
SEQ = 16384
MOST = 6144


def shared_rows(key):
    base = jnp.clip(jax.random.normal(key, (SEQ, KV_HEADS * HEAD_DIM), jnp.float32), -6.0, 6.0)
    return base


def draw_keys(key, part):
    base = shared_rows(key)
    result = base
    return result.astype(jnp.bfloat16)


def draw_queries(key, part):
    key = jax.random.fold_in(key, 1)
    result = jnp.clip(jax.random.normal(key, (SEQ, HEADS * HEAD_DIM), jnp.float32), -6.0, 6.0)
    return result.astype(jnp.bfloat16)


def block_levels(rng, shape, pieces, low, largest):
    def one(dim, parts):
        steps = jax.random.uniform(jax.random.fold_in(jax.random.fold_in(rng, 6), dim), (parts,), jnp.float32, low / len(pieces), largest / len(pieces))
        return jnp.repeat(jnp.exp(steps), shape[dim] // parts).reshape((-1,) + (1,) * (len(shape) - dim - 1))

    loudness = one(*pieces[0])
    for cut in pieces[1:]:
        loudness = loudness * one(*cut)
    return loudness


def profile(amount, total, bound, slope):
    portions = [(1 << 20) // math.isqrt(rank ** slope) + 1 for rank in range(2, amount + 1)]
    spare, counts = total - bound - (amount - 1), [1] * (amount - 1)
    while spare > 0:
        candidates = [i for i in range(amount - 1) if counts[i] < bound]
        mass, left = sum([portions[i] for i in candidates]), spare
        for i in candidates:
            more = min(bound - counts[i], max(1, left * portions[i] // mass), spare)
            counts[i] = counts[i] + more
            spare = spare - more
    return np.array([bound] + counts)


def ragged_sizes(own_key, amount, total, limit, slope):
    if amount == 2:
        one = jax.random.randint(own_key, (), max(1, total - limit), min(limit, total - 1) + 1)
        return jnp.stack([one, total - one])
    sizes = jnp.asarray(profile(amount, total, limit, slope), jnp.int32)
    pairs = (amount - 1) // 2
    giver, taker = sizes[1:1 + 2 * pairs:2], sizes[2:2 + 2 * pairs:2]
    room = jnp.minimum(giver - 1, limit - taker)
    passed = jax.random.randint(jax.random.fold_in(own_key, 1), (pairs,), 0, 1 << 20) % (room + 1)
    sizes = sizes.at[1:1 + 2 * pairs:2].set(giver - passed).at[2:2 + 2 * pairs:2].set(taker + passed)
    return sizes[jax.random.permutation(jax.random.fold_in(own_key, 2), amount)]


def noise(rng, extent, scale, most, split=(), kind=jnp.bfloat16):
    drawn = scale * jax.random.normal(rng, extent, jnp.float32)
    if split:
        drawn = drawn * block_levels(rng, extent, split, -0.22, 0.18)
    return jnp.clip(drawn, -most, most).astype(kind)


def setup_inputs(seed: int = 0) -> dict:
    key_list = jax.random.split(jax.random.key(seed), 5)
    return {
        "queries": draw_queries(jax.random.fold_in(key_list[4], 71), 0),
        "keys": draw_keys(jax.random.fold_in(key_list[4], 71), 0),
        "values": noise(key_list[2], (SEQ, KV_HEADS * HEAD_DIM), 1.0, 6.0, ((0, 128),)),
        "doc_lengths": ragged_sizes(key_list[3], NDOCS, SEQ, MOST, 2).astype(jnp.int32),
    }


def doc_starts(positions, doc_lengths):
    ends = jnp.cumsum(doc_lengths).astype(jnp.int32)
    return jnp.sum(jnp.where(ends[None, :] <= positions[:, None], doc_lengths[None, :], 0), axis=1).astype(jnp.int32)


def reference(queries, keys, values, doc_lengths):
    group = HEADS // KV_HEADS
    qblock = min(512, SEQ)
    window = min(MOST + qblock, SEQ)
    nblocks = SEQ // qblock
    positions = jnp.arange(SEQ, dtype=jnp.int32)
    starts = doc_starts(positions, doc_lengths)
    q_four = queries.reshape(SEQ, KV_HEADS, group, HEAD_DIM)
    k_three = keys.reshape(SEQ, KV_HEADS, HEAD_DIM)
    v_three = values.reshape(SEQ, KV_HEADS, HEAD_DIM)

    def one_block(index):
        q_first = (index * qblock).astype(jnp.int32)
        k_first = jnp.clip(q_first + qblock - window, 0, SEQ - window).astype(jnp.int32)
        q_blk = lax.dynamic_slice_in_dim(q_four, q_first, qblock, 0)
        k_blk = lax.dynamic_slice_in_dim(k_three, k_first, window, 0)
        v_blk = lax.dynamic_slice_in_dim(v_three, k_first, window, 0)
        q_pos = q_first + jnp.arange(qblock, dtype=jnp.int32)
        k_pos = k_first + jnp.arange(window, dtype=jnp.int32)
        q_start = lax.dynamic_slice_in_dim(starts, q_first, qblock, 0)
        visible = (k_pos[None, :] >= q_start[:, None]) & (k_pos[None, :] <= q_pos[:, None])

        def one_head(idx):
            qh = q_blk[:, idx].astype(jnp.float32)
            kh = k_blk[:, idx].astype(jnp.float32)
            vh = v_blk[:, idx].astype(jnp.float32)
            scores = jnp.einsum('qgd,wd->gqw', qh, kh) * (HEAD_DIM ** -0.5)
            masked = jnp.where(visible[None], scores, -jnp.inf)
            top = jnp.max(masked, axis=-1, keepdims=True)
            expo = jnp.where(visible[None], jnp.exp(masked - top), 0.0)
            total = jnp.sum(expo, axis=-1, keepdims=True)
            weights = expo.astype(jnp.bfloat16).astype(jnp.float32)
            return jnp.einsum('gqw,wd->qgd', weights, vh) / jnp.transpose(total, (1, 0, 2))

        heads_out = lax.map(one_head, jnp.arange(KV_HEADS, dtype=jnp.int32))
        return jnp.transpose(heads_out, (1, 0, 2, 3))

    blocks = lax.map(one_block, jnp.arange(nblocks, dtype=jnp.int32))
    return blocks.reshape(SEQ, HEADS * HEAD_DIM).astype(jnp.bfloat16)
```

```python
import functools

import jax
import jax.numpy as jnp
from jax import lax
from jax.experimental import pallas as pl
from jax.experimental.pallas import tpu as pltpu
from jax.sharding import PartitionSpec as P

MESH = pl.DeviceIdType.MESH
HEAD_DIM = 128
NDOCS = 8
NB = 16
BLK = 128
SPAN = 1024
QW = 512
KT = 256
SCALE2 = HEAD_DIM ** -0.5 * 1.4426950408889634
NEG = -1e30


def kv_head(c, j):
    return lax.rem(c // 8 + j // 4, 2) * 4 + lax.rem(c // 2, 4)


def remote(src, dst, send, recv, device):
    return pltpu.make_async_remote_copy(
        src_ref=src, dst_ref=dst, send_sem=send, recv_sem=recv, device_id=device, device_id_type=MESH
    )


def enter(peers):
    barrier = pltpu.get_barrier_semaphore()
    for peer in peers:
        pl.semaphore_signal(barrier, inc=1, device_id=peer, device_id_type=MESH)
    pl.semaphore_wait(barrier, len(peers))


def ctx_peers(c):
    core, z, y = lax.rem(c, 2), lax.rem(c // 2, 4), c // 8
    order = [(dz, dy, dc) for dy, dc in ((0, 0), (1, 1), (1, 0), (0, 1)) for dz in (2, 1, 3, 0)]
    return [
        lax.rem(y + dy, 2) * 8 + lax.rem(z + dz, 4) * 2 + lax.rem(core + dc, 2)
        for dz, dy, dc in order
        if (dz, dy, dc) != (0, 0, 0)
    ]


def gather_kernel(q_ref, k_ref, v_ref, qg_ref, kv_ref, loc, s_q, r_q, s_1, r_1, s_g, r_g, s_b, r_b, own):
    c, j = lax.axis_index("ctx"), lax.axis_index("head")
    core, x, y = lax.rem(c, 2), lax.rem(j, 4), j // 4
    sibling = {"ctx": c + 1 - 2 * core, "head": j}
    across = {"ctx": lax.rem(c + 8, 16), "head": lax.rem(j + 4, 8)}
    right = {"ctx": c, "head": y * 4 + lax.rem(x + 1, 4)}
    left = {"ctx": c, "head": y * 4 + lax.rem(x + 3, 4)}
    others = ctx_peers(c)
    for h in range(8):
        loc[0, h] = k_ref[:, h * 128 : (h + 1) * 128]
        loc[1, h] = v_ref[:, h * 128 : (h + 1) * 128].T
    enter([{"ctx": o, "head": j} for o in others] + [across, right, left])

    ends = []
    for n, o in enumerate(others):
        cp = remote(
            loc.at[lax.rem(o, 2), kv_head(o, j)], kv_ref.at[lax.rem(o, 2), c, j],
            s_1.at[n], r_1.at[n], {"ctx": o, "head": j},
        )
        cp.start()
        ends.append(cp)
    mine = pltpu.make_async_copy(loc.at[core, kv_head(c, j)], kv_ref.at[core, c, j], own.at[0])
    mine.start()
    q_ends = []
    for n, o in enumerate(others):
        columns = kv_head(o, j) * 1024 + lax.rem(o, 2) * QW
        cp = remote(
            q_ref.at[:, pl.ds(pl.multiple_of(columns, QW), QW)], qg_ref.at[c],
            s_q.at[n], r_q.at[n], {"ctx": o, "head": j},
        )
        cp.start()
        q_ends.append(cp)
    columns = kv_head(c, j) * 1024 + core * QW
    mine_q = pltpu.make_async_copy(q_ref.at[:, pl.ds(pl.multiple_of(columns, QW), QW)], qg_ref.at[c], own.at[1])
    mine_q.start()
    mine.wait()
    for cp in ends:
        cp.wait_recv()

    def slot(dx, dy, half=None):
        place = lax.rem(y + dy, 2) * 4 + lax.rem(x + dx, 4)
        if half is None:
            return kv_ref.at[core, :, place]
        return kv_ref.at[core, pl.ds(half * 8, 8), place]

    count = [0]
    to_sibling = []

    def go(ref, device):
        cp = remote(ref, ref, s_g.at[count[0]], r_g.at[count[0]], device)
        count[0] += 1
        cp.start()
        return cp

    def give(ref):
        n = len(to_sibling)
        cp = remote(ref, ref, s_b.at[n], r_b.at[n], sibling)
        cp.start()
        to_sibling.append(cp)

    hops = []
    over = go(slot(0, 0), across)
    first = [(go(slot(0, 0), right), go(slot(0, 0), left))]
    give(slot(0, 0))
    over.wait_recv()
    first.append((go(slot(0, 1), right), go(slot(0, 1), left)))
    give(slot(0, 1))
    second = []
    for dy in (0, 1):
        from_left, from_right = first[dy]
        from_left.wait_recv()
        a = go(slot(3, dy, 0), right)
        give(slot(3, dy))
        from_right.wait_recv()
        b = go(slot(1, dy, 1), left)
        give(slot(1, dy))
        second.append((a, b))
        hops += [from_left, from_right, a, b]
    for dy in (0, 1):
        a, b = second[dy]
        a.wait_recv()
        b.wait_recv()
        give(slot(2, dy))
    mine_q.wait()
    for cp in q_ends:
        cp.wait()
    for cp in ends + [over] + hops:
        cp.wait_send()
    for cp in to_sibling:
        cp.wait()


def gather(q, k, v):
    dma = pltpu.SemaphoreType.DMA
    anywhere, vmem = pl.BlockSpec(memory_space=pl.ANY), pl.BlockSpec(memory_space=pltpu.VMEM)
    return pl.pallas_call(
        gather_kernel,
        out_shape=(
            jax.ShapeDtypeStruct((NB, BLK, QW), jnp.bfloat16),
            jax.ShapeDtypeStruct((2, NB, 8, BLK, HEAD_DIM), jnp.bfloat16),
        ),
        in_specs=[anywhere, vmem, vmem],
        out_specs=(anywhere, anywhere),
        scratch_shapes=[
            pltpu.VMEM((2, 8, BLK, HEAD_DIM), jnp.bfloat16),
            dma((15,)), dma((15,)), dma((15,)), dma((15,)), dma((9,)), dma((9,)), dma((8,)), dma((8,)), dma((2,)),
        ],
        compiler_params=pltpu.CompilerParams(collective_id=0, has_side_effects=True),
    )(q, k, v)


def attend_kernel(lengths, q_ref, kv_ref, o_ref, m_ref, a_ref, st_ref, lo_ref, s0, s1, p0, p1, al0, al1):
    sb, pb, ab = (s0, s1), (p0, p1), (al0, al1)
    core, j = lax.rem(lax.axis_index("ctx"), 2), lax.axis_index("head")
    halves, width = 2, QW // 2
    m_ref[...] = jnp.full(m_ref.shape, NEG, jnp.float32)
    a_ref[...] = jnp.zeros(a_ref.shape, jnp.float32)
    p1[...] = jnp.zeros(p1.shape, jnp.bfloat16)
    al1[...] = jnp.zeros(al1.shape, jnp.float32)
    total = jnp.int32(0)
    for i in range(NB):
        p = i * SPAN + j * BLK
        row = lax.broadcasted_iota(jnp.int32, (1, BLK), 1) + p
        start, low, end = jnp.zeros((1, BLK), jnp.int32), jnp.int32(0), jnp.int32(0)
        for d in range(NDOCS - 1):
            end = end + lengths[d]
            start = jnp.where(row >= end, end, start)
            low = jnp.where(p >= end, end, low)
        st_ref[i] = start
        lo_ref[i] = low
        total = total + (p + BLK - low + KT - 1) // KT

    def after(b, top):
        low = top - KT
        done = low <= lo_ref[b]
        following = jnp.minimum(b + 1, NB - 1)
        finished = (done & (b + 1 >= NB)) | (top < 0)
        new_top = jnp.where(done, following * SPAN + j * BLK + BLK, low)
        return jnp.where(done, following, b), jnp.where(finished, -1, new_top)

    def first_block(top):
        return jnp.maximum(top - KT, 0) // BLK

    def scores(b, top, s_ref, n):
        k = kv_ref[0, pl.ds(first_block(top), KT // BLK)].reshape(KT, HEAD_DIM)
        q = jnp.concatenate([q_ref[b, :, h * 128 : (h + 1) * 128] for h in (2 * n, 2 * n + 1)], 0)
        s_ref[:, n * width : (n + 1) * width] = lax.dot_general(
            k, q, (((1,), (1,)), ((), ())), preferred_element_type=jnp.float32
        )

    def visible(b, top):
        k_first = first_block(top) * BLK
        row = lax.broadcasted_iota(jnp.int32, (1, BLK), 1) + (b * SPAN + j * BLK)
        last = jnp.minimum(row, top - 1) - k_first
        place = lax.broadcasted_iota(jnp.int32, (KT, BLK), 0)
        return (place >= st_ref[b] - k_first) & (place <= last)

    def weights(b, s_ref, p_ref, f_ref, n, seen):
        part = slice(n * width, (n + 1) * width)
        s = s_ref[:, part]
        s = jnp.concatenate([jnp.where(seen, s[:, h * 128 : (h + 1) * 128], NEG) for h in (0, 1)], 1)
        old = m_ref[b, :, part]
        new = jnp.maximum(old, jnp.max(s, axis=0, keepdims=True))
        p_ref[:, part] = jnp.exp2((s - new) * SCALE2).astype(jnp.bfloat16)
        f_ref[:, part] = jnp.exp2((old - new) * SCALE2)
        m_ref[b, :, part] = new

    def mix(b, top, p_ref, f_ref, n):
        part = slice(n * width, (n + 1) * width)
        base = first_block(top)
        vt = jnp.concatenate([kv_ref[1, base + t] for t in range(KT // BLK)], 1)
        vt = jnp.concatenate([vt, jnp.ones((16, KT), jnp.bfloat16)], 0)
        product = jnp.dot(vt, p_ref[:, part], preferred_element_type=jnp.float32)
        a_ref[b, :, part] = a_ref[b, :, part] * f_ref[:, part] + product

    b0, top0 = jnp.int32(0), j * BLK + BLK
    for n in range(halves):
        scores(b0, top0, sb[0], n)

    def body(_, carry):
        b_old, top_old, b, top = carry
        for u in range(4):
            now, other = u % 2, (u + 1) % 2
            b_new, top_new = after(b, top)
            seen = visible(b, top)
            for n in range(halves):
                scores(b_new, top_new, sb[other], n)
                weights(b, sb[now], pb[now], ab[now], n, seen)
                mix(b_old, top_old, pb[other], ab[other], n)
            b_old, top_old, b, top = b, top, b_new, top_new
        return b_old, top_old, b, top

    lax.fori_loop(0, (total + 4) // 4, body, (b0, top0, b0, top0))

    def finish(i, _):
        out = a_ref[i, 0:128] / a_ref[i, 128:129]
        for h in range(4):
            o_ref[i, :, h * 128 : (h + 1) * 128] = out[:, h * 128 : (h + 1) * 128].T.astype(jnp.bfloat16)
        return 0

    lax.fori_loop(0, NB, finish, 0)


def attend(lengths, q, kv):
    f32, vmem = jnp.float32, pltpu.VMEM
    return pl.pallas_call(
        attend_kernel,
        out_shape=jax.ShapeDtypeStruct((NB, BLK, QW), jnp.bfloat16),
        grid_spec=pltpu.PrefetchScalarGridSpec(
            num_scalar_prefetch=1,
            grid=(),
            in_specs=[pl.BlockSpec(memory_space=vmem)] * 2,
            out_specs=pl.BlockSpec(memory_space=vmem),
            scratch_shapes=[
                vmem((NB, 1, QW), f32),
                vmem((NB, 144, QW), f32),
                vmem((NB, 1, BLK), jnp.int32),
                pltpu.SMEM((NB,), jnp.int32),
                vmem((KT, QW), f32),
                vmem((KT, QW), f32),
                vmem((KT, QW), jnp.bfloat16),
                vmem((KT, QW), jnp.bfloat16),
                vmem((1, QW), f32),
                vmem((1, QW), f32),
            ],
        ),
        compiler_params=pltpu.CompilerParams(vmem_limit_bytes=48 * 2**20),
    )(lengths, q, kv)


def return_kernel(o_ref, out_ref, send, recv, own):
    c, j = lax.axis_index("ctx"), lax.axis_index("head")
    others = ctx_peers(c)
    enter([{"ctx": o, "head": j} for o in others])
    columns = pl.ds(pl.multiple_of(kv_head(c, j) * 1024 + lax.rem(c, 2) * QW, QW), QW)
    ends = []
    for n, o in enumerate(others):
        cp = remote(o_ref.at[o], out_ref.at[:, columns], send.at[n], recv.at[n], {"ctx": o, "head": j})
        cp.start()
        ends.append(cp)
    mine = pltpu.make_async_copy(o_ref.at[c], out_ref.at[:, columns], own)
    mine.start()
    mine.wait()
    for cp in ends:
        cp.wait()


def give_back(o):
    dma = pltpu.SemaphoreType.DMA
    anywhere = pl.BlockSpec(memory_space=pl.ANY)
    return pl.pallas_call(
        return_kernel,
        out_shape=jax.ShapeDtypeStruct((BLK, 64 * HEAD_DIM), jnp.bfloat16),
        in_specs=[anywhere],
        out_specs=anywhere,
        scratch_shapes=[dma((15,)), dma((15,)), dma],
        compiler_params=pltpu.CompilerParams(collective_id=1, has_side_effects=True),
    )(o)


def on_device(queries, keys, values, doc_lengths):
    q, kv = gather(queries, keys, values)
    o = attend(doc_lengths, q, kv.reshape(2, NB * 8, BLK, HEAD_DIM))
    return give_back(o)


def solution(mesh):
    rows = P(("ctx", "head"), None)
    return jax.shard_map(on_device, mesh=mesh, in_specs=(rows, rows, rows, P()), out_specs=rows, check_vma=False)
```

```python
import functools

import jax
import jax.numpy as jnp
from jax import lax
from jax.experimental import pallas as pl
from jax.experimental.pallas import tpu as pltpu
from jax.sharding import PartitionSpec as P

MESH = pl.DeviceIdType.MESH
HEAD_DIM = 128
NDOCS = 8
NB = 16
BLK = 128
SPAN = 1024
QW = 512
KT = 512
DIAG = 4
SCALE2 = HEAD_DIM ** -0.5 * 1.4426950408889634
NEG = -1e30


def kv_head(c, j):
    return lax.rem(c // 8 + j // 4, 2) * 4 + lax.rem(c // 2, 4)


def remote(src, dst, send, recv, device):
    return pltpu.make_async_remote_copy(
        src_ref=src, dst_ref=dst, send_sem=send, recv_sem=recv, device_id=device, device_id_type=MESH
    )


def enter(peers):
    barrier = pltpu.get_barrier_semaphore()
    for peer in peers:
        pl.semaphore_signal(barrier, inc=1, device_id=peer, device_id_type=MESH)
    pl.semaphore_wait(barrier, len(peers))


def ctx_peers(c):
    core, z, y = lax.rem(c, 2), lax.rem(c // 2, 4), c // 8
    order = [(dz, dy, dc) for dy, dc in ((0, 0), (1, 1), (1, 0), (0, 1)) for dz in (2, 1, 3, 0)]
    return [
        lax.rem(y + dy, 2) * 8 + lax.rem(z + dz, 4) * 2 + lax.rem(core + dc, 2)
        for dz, dy, dc in order
        if (dz, dy, dc) != (0, 0, 0)
    ]


def gather_kernel(q_ref, k_ref, v_ref, qg_ref, kv_ref, loc, s_q, r_q, s_1, r_1, s_g, r_g, s_b, r_b, own):
    c, j = lax.axis_index("ctx"), lax.axis_index("head")
    core, x, y = lax.rem(c, 2), lax.rem(j, 4), j // 4
    sibling = {"ctx": c + 1 - 2 * core, "head": j}
    across = {"ctx": lax.rem(c + 8, 16), "head": lax.rem(j + 4, 8)}
    right = {"ctx": c, "head": y * 4 + lax.rem(x + 1, 4)}
    left = {"ctx": c, "head": y * 4 + lax.rem(x + 3, 4)}
    others = ctx_peers(c)
    for h in range(8):
        loc[0, h] = k_ref[:, h * 128 : (h + 1) * 128]
        loc[1, h] = v_ref[:, h * 128 : (h + 1) * 128].T
    enter([{"ctx": o, "head": j} for o in others] + [across, right, left])

    ends = []
    for n, o in enumerate(others):
        cp = remote(
            loc.at[lax.rem(o, 2), kv_head(o, j)], kv_ref.at[lax.rem(o, 2), c, j],
            s_1.at[n], r_1.at[n], {"ctx": o, "head": j},
        )
        cp.start()
        ends.append(cp)
    mine = pltpu.make_async_copy(loc.at[core, kv_head(c, j)], kv_ref.at[core, c, j], own.at[0])
    mine.start()
    columns = kv_head(c, j) * 1024 + core * QW
    mine_q = pltpu.make_async_copy(q_ref.at[:, pl.ds(pl.multiple_of(columns, QW), QW)], qg_ref.at[c], own.at[1])
    mine_q.start()
    mine.wait()
    for cp in ends:
        cp.wait_recv()

    def part(dx, dy, first, size):
        place = lax.rem(y + dy, 2) * 4 + lax.rem(x + dx, 4)
        return kv_ref.at[core, pl.ds(first, size), place]

    moves, to_sibling = [], []

    def go(ref, device):
        n = len(moves)
        cp = remote(ref, ref, s_g.at[n], r_g.at[n], device)
        cp.start()
        moves.append(cp)
        return cp

    def give(ref):
        n = len(to_sibling)
        cp = remote(ref, ref, s_b.at[n], r_b.at[n], sibling)
        cp.start()
        to_sibling.append(cp)

    a_over = go(part(0, 0, 0, 8), across)
    a_right, a_left = go(part(0, 0, 0, 8), right), go(part(0, 0, 0, 8), left)
    b_right, b_left = go(part(0, 0, 8, 8), right), go(part(0, 0, 8, 8), left)
    b_over = go(part(0, 0, 8, 8), across)
    give(part(0, 0, 0, 16))
    q_ends = []
    for n, o in enumerate(others):
        columns = kv_head(o, j) * 1024 + lax.rem(o, 2) * QW
        cp = remote(
            q_ref.at[:, pl.ds(pl.multiple_of(columns, QW), QW)], qg_ref.at[c],
            s_q.at[n], r_q.at[n], {"ctx": o, "head": j},
        )
        cp.start()
        q_ends.append(cp)
    a_over.wait_recv()
    c_right, c_left = go(part(0, 1, 0, 8), right), go(part(0, 1, 0, 8), left)
    a_right.wait_recv()
    a_far_right = go(part(3, 0, 0, 4), right)
    a_left.wait_recv()
    a_far_left = go(part(1, 0, 4, 4), left)
    b_right.wait_recv()
    b_far_right = go(part(3, 0, 8, 4), right)
    b_over_3 = go(part(3, 0, 8, 8), across)
    give(part(3, 0, 0, 16))
    b_left.wait_recv()
    b_far_left = go(part(1, 0, 12, 4), left)
    b_over_1 = go(part(1, 0, 8, 8), across)
    give(part(1, 0, 0, 16))
    b_over.wait_recv()
    give(part(0, 1, 0, 16))
    c_right.wait_recv()
    c_far_right = go(part(3, 1, 0, 4), right)
    c_left.wait_recv()
    c_far_left = go(part(1, 1, 4, 4), left)
    b_far_right.wait_recv()
    b_far_left.wait_recv()
    b_over_2 = go(part(2, 0, 8, 8), across)
    a_far_right.wait_recv()
    a_far_left.wait_recv()
    give(part(2, 0, 0, 16))
    b_over_3.wait_recv()
    give(part(3, 1, 0, 16))
    b_over_1.wait_recv()
    give(part(1, 1, 0, 16))
    c_far_right.wait_recv()
    c_far_left.wait_recv()
    b_over_2.wait_recv()
    give(part(2, 1, 0, 16))
    mine_q.wait()
    for cp in q_ends:
        cp.wait()
    for cp in ends + moves:
        cp.wait_send()
    for cp in to_sibling:
        cp.wait()


def gather(q, k, v):
    dma = pltpu.SemaphoreType.DMA
    anywhere, vmem = pl.BlockSpec(memory_space=pl.ANY), pl.BlockSpec(memory_space=pltpu.VMEM)
    return pl.pallas_call(
        gather_kernel,
        out_shape=(
            jax.ShapeDtypeStruct((NB, BLK, QW), jnp.bfloat16),
            jax.ShapeDtypeStruct((2, NB, 8, BLK, HEAD_DIM), jnp.bfloat16),
        ),
        in_specs=[anywhere, vmem, vmem],
        out_specs=(anywhere, anywhere),
        scratch_shapes=[
            pltpu.VMEM((2, 8, BLK, HEAD_DIM), jnp.bfloat16),
            dma((15,)), dma((15,)), dma((15,)), dma((15,)), dma((17,)), dma((17,)), dma((8,)), dma((8,)), dma((2,)),
        ],
        compiler_params=pltpu.CompilerParams(collective_id=0, has_side_effects=True),
    )(q, k, v)


def attend_kernel(
    lengths, q_hbm, kv_ref, o_hbm, q_ref, o_ref, kd, vd, kb, vb, ka, qa, m_ref, a_ref, lo_ref, next_ref,
    s0, s1, p0, p1, f0, f1, x0, x1, load, store,
):
    sb, pb, fb, xb = (s0, s1), (p0, p1), (f0, f1), (x0, x1)
    j = lax.axis_index("head")
    bf = jnp.bfloat16
    copies = [
        pltpu.make_async_copy(q_hbm, q_ref, load.at[0]),
        pltpu.make_async_copy(kv_ref.at[0, :, j], kd, load.at[1]),
        pltpu.make_async_copy(kv_ref.at[1, :, j], vd, load.at[2]),
        pltpu.make_async_copy(kv_ref.at[0], kb.at[pl.ds(1, NB)], load.at[3]),
        pltpu.make_async_copy(kv_ref.at[1], vb.at[pl.ds(1, NB)], load.at[4]),
    ]
    for cp in copies:
        cp.start()

    lane = lax.broadcasted_iota(jnp.int32, (1, BLK), 1)
    first, last, end, ends = jnp.zeros((1, BLK), jnp.int32), jnp.full((1, BLK), 1 << 30, jnp.int32), jnp.int32(0), []
    for d in range(NDOCS):
        first = jnp.where(lane == d, end, first)
        end = end + lengths[d]
        ends.append(end)
        last = jnp.where(lane == d, end, last)
    place = lax.broadcasted_iota(jnp.int32, (BLK, BLK), 0)
    kb[0] = jnp.zeros(kb.shape[1:], bf)
    vb[0] = jnp.zeros(vb.shape[1:], bf)
    ka[0] = jnp.full(ka.shape[1:], NEG, bf)

    def mark(i, _):
        for t in range(8):
            row = place + (i * SPAN + t * BLK)
            ka[i + 1, t] = jnp.where((row >= first) & (row < last), 0.0, NEG).astype(bf)
        return 0

    lax.fori_loop(0, NB, mark, 0)
    total = jnp.int32(0)
    for i in range(NB):
        p = i * SPAN + j * BLK
        row = place + p
        qa[i] = jnp.where((row >= first) & (row < last), 1.0, 0.0).astype(bf)
        low = jnp.int32(0)
        for d in range(NDOCS - 1):
            low = jnp.where(p >= ends[d], ends[d], low)
        lo_ref[i] = low
        total = total + (p - low + KT - 1) // KT
    follow = jnp.int32(NB - 1)
    for i in range(NB - 1, -1, -1):
        next_ref[i] = follow
        follow = jnp.where(i * SPAN + j * BLK > lo_ref[i], i, follow)
    p1[...] = jnp.zeros(p1.shape, bf)
    f1[...] = jnp.ones(f1.shape, jnp.float32)

    def queries(b):
        marks = qa[b]
        return jnp.concatenate(
            [jnp.concatenate([q_ref[b, :, h * 128 : (h + 1) * 128], marks], 1) for h in range(4)], 0
        )

    def product(k, q):
        return lax.dot_general(k, q, (((1,), (1,)), ((), ())), preferred_element_type=jnp.float32)

    def with_ones(vt):
        return jnp.concatenate([vt, jnp.ones((16, vt.shape[1]), bf)], 0)

    for cp in copies[:3]:
        cp.wait()
    below = place <= lax.broadcasted_iota(jnp.int32, (BLK, BLK), 1)

    def diagonal(g, _):
        blocks = [g * DIAG + u for u in range(DIAG)]
        scores = []
        for b in blocks:
            s = product(jnp.concatenate([kd[b], ka[b + 1, j]], 1), queries(b))
            scores.append(jnp.concatenate([jnp.where(below, s[:, h * 128 : (h + 1) * 128], NEG) for h in range(4)], 1))
        parts = []
        for b, s in zip(blocks, scores):
            top = jnp.max(s, axis=0, keepdims=True)
            m_ref[b] = top
            parts.append(jnp.exp2((s - top) * SCALE2).astype(bf))
        for b, p in zip(blocks, parts):
            a_ref[b] = jnp.dot(with_ones(vd[b]), p, preferred_element_type=jnp.float32)
        return 0

    lax.fori_loop(0, NB // DIAG, diagonal, 0)
    for cp in copies[3:]:
        cp.wait()

    kf, af, vf = (r.reshape((NB + 1) * 8, BLK, HEAD_DIM) for r in (kb, ka, vb))
    steps = KT // BLK

    def after(b, top):
        low = top - KT
        done = low <= lo_ref[b]
        b_new = jnp.where(done, next_ref[b], b)
        over = (done & (b_new <= b)) | (top <= 0)
        return b_new, jnp.where(over, 0, jnp.where(done, b_new * SPAN + j * BLK, low))

    def window(top):
        return (jnp.maximum(top, 0) - KT + SPAN) // BLK

    def score(b, top, s_ref, x_ref):
        at = pl.ds(window(top), steps)
        k = jnp.concatenate([kf[at].reshape(KT, HEAD_DIM), af[at].reshape(KT, BLK)], 1)
        s = product(k, queries(b))
        s_ref[...] = s
        x_ref[...] = jnp.max(s, axis=0, keepdims=True)

    def weigh(b, s_ref, x_ref, p_ref, f_ref):
        old = m_ref[b]
        new = jnp.maximum(old, x_ref[...])
        p_ref[...] = jnp.exp2((s_ref[...] - new) * SCALE2).astype(bf)
        f_ref[...] = jnp.exp2((old - new) * SCALE2)
        m_ref[b] = new

    def mix(b, top, p_ref, f_ref):
        at = window(top)
        vt = jnp.concatenate([vf[at + t] for t in range(steps)], 1)
        a_ref[b] = a_ref[b] * f_ref[...] + jnp.dot(with_ones(vt), p_ref[...], preferred_element_type=jnp.float32)

    b0, top0 = follow, follow * SPAN + j * BLK
    score(b0, top0, sb[0], xb[0])

    def body(_, carry):
        b_old, top_old, b, top = carry
        for u in range(4):
            now, other = u % 2, (u + 1) % 2
            b_new, top_new = after(b, top)
            weigh(b, sb[now], xb[now], pb[now], fb[now])
            mix(b_old, top_old, pb[other], fb[other])
            score(b_new, top_new, sb[other], xb[other])
            b_old, top_old, b, top = b, top, b_new, top_new
        return b_old, top_old, b, top

    lax.fori_loop(0, jnp.where(total > 0, (total + 4) // 4, 0), body, (b0, top0, b0, top0))

    def finish(i, _):
        out = a_ref[i, 0:128] * (1.0 / a_ref[i, 128:129])
        for h in range(4):
            o_ref[i, :, h * 128 : (h + 1) * 128] = out[:, h * 128 : (h + 1) * 128].T.astype(bf)
        pltpu.make_async_copy(o_ref.at[i], o_hbm.at[i], store.at[i]).start()
        return 0

    lax.fori_loop(0, NB, finish, 0)
    for i in range(NB):
        pltpu.make_async_copy(o_ref.at[i], o_hbm.at[i], store.at[i]).wait()


def attend(lengths, q, kv):
    f32, bf, vmem = jnp.float32, jnp.bfloat16, pltpu.VMEM
    anywhere = pl.BlockSpec(memory_space=pl.ANY)
    return pl.pallas_call(
        attend_kernel,
        out_shape=jax.ShapeDtypeStruct((NB, BLK, QW), bf),
        grid_spec=pltpu.PrefetchScalarGridSpec(
            num_scalar_prefetch=1,
            grid=(),
            in_specs=[anywhere] * 2,
            out_specs=anywhere,
            scratch_shapes=[
                vmem((NB, BLK, QW), bf),
                vmem((NB, BLK, QW), bf),
                vmem((NB, BLK, HEAD_DIM), bf),
                vmem((NB, HEAD_DIM, BLK), bf),
                vmem((NB + 1, 8, BLK, HEAD_DIM), bf),
                vmem((NB + 1, 8, HEAD_DIM, BLK), bf),
                vmem((NB + 1, 8, BLK, BLK), bf),
                vmem((NB, BLK, BLK), bf),
                vmem((NB, 1, QW), f32),
                vmem((NB, 144, QW), f32),
                pltpu.SMEM((NB,), jnp.int32),
                pltpu.SMEM((NB,), jnp.int32),
                vmem((KT, QW), f32),
                vmem((KT, QW), f32),
                vmem((KT, QW), bf),
                vmem((KT, QW), bf),
                vmem((1, QW), f32),
                vmem((1, QW), f32),
                vmem((1, QW), f32),
                vmem((1, QW), f32),
                pltpu.SemaphoreType.DMA((5,)),
                pltpu.SemaphoreType.DMA((NB,)),
            ],
        ),
        compiler_params=pltpu.CompilerParams(vmem_limit_bytes=56 * 2**20),
    )(lengths, q, kv)


def return_kernel(o_ref, out_ref, send, recv, own):
    c, j = lax.axis_index("ctx"), lax.axis_index("head")
    others = ctx_peers(c)
    enter([{"ctx": o, "head": j} for o in others])
    columns = pl.ds(pl.multiple_of(kv_head(c, j) * 1024 + lax.rem(c, 2) * QW, QW), QW)
    ends = []
    for n, o in enumerate(others):
        cp = remote(o_ref.at[o], out_ref.at[:, columns], send.at[n], recv.at[n], {"ctx": o, "head": j})
        cp.start()
        ends.append(cp)
    mine = pltpu.make_async_copy(o_ref.at[c], out_ref.at[:, columns], own)
    mine.start()
    mine.wait()
    for cp in ends:
        cp.wait()


def give_back(o):
    dma = pltpu.SemaphoreType.DMA
    anywhere = pl.BlockSpec(memory_space=pl.ANY)
    return pl.pallas_call(
        return_kernel,
        out_shape=jax.ShapeDtypeStruct((BLK, 64 * HEAD_DIM), jnp.bfloat16),
        in_specs=[anywhere],
        out_specs=anywhere,
        scratch_shapes=[dma((15,)), dma((15,)), dma],
        compiler_params=pltpu.CompilerParams(collective_id=1, has_side_effects=True),
    )(o)


def on_device(queries, keys, values, doc_lengths):
    q, kv = gather(queries, keys, values)
    o = attend(doc_lengths, q, kv)
    return give_back(o)


def solution(mesh):
    rows = P(("ctx", "head"), None)
    return jax.shard_map(on_device, mesh=mesh, in_specs=(rows, rows, rows, P()), out_specs=rows, check_vma=False)
```

```python
import functools

import jax
import jax.numpy as jnp
from jax import lax
from jax.experimental import pallas as pl
from jax.experimental.pallas import tpu as pltpu
from jax.sharding import PartitionSpec as P

MESH = pl.DeviceIdType.MESH
HEAD_DIM = 128
NDOCS = 8
NB = 16
BLK = 128
SPAN = 1024
QW = 512
KT = 512
NEAR = 7 * 128
UNROLL = 1
SCALE2 = HEAD_DIM ** -0.5 * 1.4426950408889634
NEG = -1e30


def kv_head(c, j):
    return lax.rem(c // 8 + j // 4, 2) * 4 + lax.rem(c // 2, 4)


def remote(src, dst, send, recv, device):
    return pltpu.make_async_remote_copy(
        src_ref=src, dst_ref=dst, send_sem=send, recv_sem=recv, device_id=device, device_id_type=MESH
    )


def enter(peers):
    barrier = pltpu.get_barrier_semaphore()
    for peer in peers:
        pl.semaphore_signal(barrier, inc=1, device_id=peer, device_id_type=MESH)
    pl.semaphore_wait(barrier, len(peers))


def ctx_peers(c):
    core, z, y = lax.rem(c, 2), lax.rem(c // 2, 4), c // 8
    order = [(dz, dy, dc) for dy, dc in ((0, 0), (1, 1), (1, 0), (0, 1)) for dz in (2, 1, 3, 0)]
    return [
        lax.rem(y + dy, 2) * 8 + lax.rem(z + dz, 4) * 2 + lax.rem(core + dc, 2)
        for dz, dy, dc in order
        if (dz, dy, dc) != (0, 0, 0)
    ]


def gather_kernel(q_ref, k_ref, v_ref, qg_ref, kv_ref, loc, s_q, r_q, s_1, r_1, s_g, r_g, s_b, r_b, own):
    c, j = lax.axis_index("ctx"), lax.axis_index("head")
    core, x, y = lax.rem(c, 2), lax.rem(j, 4), j // 4
    sibling = {"ctx": c + 1 - 2 * core, "head": j}
    across = {"ctx": lax.rem(c + 8, 16), "head": lax.rem(j + 4, 8)}
    right = {"ctx": c, "head": y * 4 + lax.rem(x + 1, 4)}
    left = {"ctx": c, "head": y * 4 + lax.rem(x + 3, 4)}
    others = ctx_peers(c)
    for h in range(8):
        loc[0, h] = k_ref[:, h * 128 : (h + 1) * 128]
        loc[1, h] = v_ref[:, h * 128 : (h + 1) * 128].T
    enter([{"ctx": o, "head": j} for o in others] + [across, right, left])

    ends = []
    for n, o in enumerate(others):
        cp = remote(
            loc.at[lax.rem(o, 2), kv_head(o, j)], kv_ref.at[lax.rem(o, 2), c, j],
            s_1.at[n], r_1.at[n], {"ctx": o, "head": j},
        )
        cp.start()
        ends.append(cp)
    mine = pltpu.make_async_copy(loc.at[core, kv_head(c, j)], kv_ref.at[core, c, j], own.at[0])
    mine.start()
    columns = kv_head(c, j) * 1024 + core * QW
    mine_q = pltpu.make_async_copy(q_ref.at[:, pl.ds(pl.multiple_of(columns, QW), QW)], qg_ref.at[c], own.at[1])
    mine_q.start()
    mine.wait()
    for cp in ends:
        cp.wait_recv()

    def part(dx, dy, first, size):
        place = lax.rem(y + dy, 2) * 4 + lax.rem(x + dx, 4)
        return kv_ref.at[core, pl.ds(first, size), place]

    moves, to_sibling = [], []

    def go(ref, device):
        n = len(moves)
        cp = remote(ref, ref, s_g.at[n], r_g.at[n], device)
        cp.start()
        moves.append(cp)
        return cp

    def give(ref):
        n = len(to_sibling)
        cp = remote(ref, ref, s_b.at[n], r_b.at[n], sibling)
        cp.start()
        to_sibling.append(cp)

    a_over = go(part(0, 0, 0, 8), across)
    a_right, a_left = go(part(0, 0, 0, 8), right), go(part(0, 0, 0, 8), left)
    b_right, b_left = go(part(0, 0, 8, 8), right), go(part(0, 0, 8, 8), left)
    b_over = go(part(0, 0, 8, 8), across)
    give(part(0, 0, 0, 16))
    q_ends = []
    for n, o in enumerate(others):
        columns = kv_head(o, j) * 1024 + lax.rem(o, 2) * QW
        cp = remote(
            q_ref.at[:, pl.ds(pl.multiple_of(columns, QW), QW)], qg_ref.at[c],
            s_q.at[n], r_q.at[n], {"ctx": o, "head": j},
        )
        cp.start()
        q_ends.append(cp)
    a_over.wait_recv()
    c_right, c_left = go(part(0, 1, 0, 8), right), go(part(0, 1, 0, 8), left)
    a_right.wait_recv()
    a_far_right = go(part(3, 0, 0, 4), right)
    a_left.wait_recv()
    a_far_left = go(part(1, 0, 4, 4), left)
    b_right.wait_recv()
    b_far_right = go(part(3, 0, 8, 4), right)
    b_over_3 = go(part(3, 0, 8, 8), across)
    give(part(3, 0, 0, 16))
    b_left.wait_recv()
    b_far_left = go(part(1, 0, 12, 4), left)
    b_over_1 = go(part(1, 0, 8, 8), across)
    give(part(1, 0, 0, 16))
    b_over.wait_recv()
    give(part(0, 1, 0, 16))
    c_right.wait_recv()
    c_far_right = go(part(3, 1, 0, 4), right)
    c_left.wait_recv()
    c_far_left = go(part(1, 1, 4, 4), left)
    b_far_right.wait_recv()
    b_far_left.wait_recv()
    b_over_2 = go(part(2, 0, 8, 8), across)
    a_far_right.wait_recv()
    a_far_left.wait_recv()
    give(part(2, 0, 0, 16))
    b_over_3.wait_recv()
    give(part(3, 1, 0, 16))
    b_over_1.wait_recv()
    give(part(1, 1, 0, 16))
    c_far_right.wait_recv()
    c_far_left.wait_recv()
    b_over_2.wait_recv()
    give(part(2, 1, 0, 16))
    mine_q.wait()
    for cp in q_ends:
        cp.wait()
    for cp in ends + moves:
        cp.wait_send()
    for cp in to_sibling:
        cp.wait()


def gather(q, k, v):
    dma = pltpu.SemaphoreType.DMA
    anywhere, vmem = pl.BlockSpec(memory_space=pl.ANY), pl.BlockSpec(memory_space=pltpu.VMEM)
    return pl.pallas_call(
        gather_kernel,
        out_shape=(
            jax.ShapeDtypeStruct((NB, BLK, QW), jnp.bfloat16),
            jax.ShapeDtypeStruct((2, NB, 8, BLK, HEAD_DIM), jnp.bfloat16),
        ),
        in_specs=[anywhere, vmem, vmem],
        out_specs=(anywhere, anywhere),
        scratch_shapes=[
            pltpu.VMEM((2, 8, BLK, HEAD_DIM), jnp.bfloat16),
            dma((15,)), dma((15,)), dma((15,)), dma((15,)), dma((17,)), dma((17,)), dma((8,)), dma((8,)), dma((2,)),
        ],
        compiler_params=pltpu.CompilerParams(collective_id=0, has_side_effects=True),
    )(q, k, v)


def attend_kernel(
    lengths, q_hbm, kv_ref, m_hbm, a_hbm, q_ref, kb, vb, ka, qa, m_ref, a_ref, lo_ref, next_ref,
    s0, s1, p0, p1, f0, f1, x0, x1, load, store,
):
    sb, pb, fb, xb = (s0, s1), (p0, p1), (f0, f1), (x0, x1)
    j = lax.axis_index("head")
    bf = jnp.bfloat16
    copies = [
        pltpu.make_async_copy(q_hbm, q_ref, load.at[0]),
        pltpu.make_async_copy(kv_ref.at[0], kb.at[pl.ds(1, NB)], load.at[1]),
        pltpu.make_async_copy(kv_ref.at[1], vb.at[pl.ds(1, NB)], load.at[2]),
    ]
    for cp in copies:
        cp.start()

    lane = lax.broadcasted_iota(jnp.int32, (1, BLK), 1)
    first, last, end, ends = jnp.zeros((1, BLK), jnp.int32), jnp.full((1, BLK), 1 << 30, jnp.int32), jnp.int32(0), []
    for d in range(NDOCS):
        first = jnp.where(lane == d, end, first)
        end = end + lengths[d]
        ends.append(end)
        last = jnp.where(lane == d, end, last)
    place = lax.broadcasted_iota(jnp.int32, (BLK, BLK), 0)
    kb[0] = jnp.zeros(kb.shape[1:], bf)
    vb[0] = jnp.zeros(vb.shape[1:], bf)
    ka[0] = jnp.full(ka.shape[1:], NEG, bf)

    def mark(i, _):
        for t in range(8):
            row = place + (i * SPAN + t * BLK)
            ka[i + 1, t] = jnp.where((row >= first) & (row < last), 0.0, NEG).astype(bf)
        return 0

    lax.fori_loop(0, NB, mark, 0)
    total = jnp.int32(0)
    for i in range(NB):
        p = i * SPAN + j * BLK
        row = place + p
        qa[i] = jnp.where((row >= first) & (row < last), 1.0, 0.0).astype(bf)
        low = jnp.int32(0)
        for d in range(NDOCS - 1):
            low = jnp.where(p >= ends[d], ends[d], low)
        lo_ref[i] = low
        total = total + jnp.maximum(p - NEAR - low + KT - 1, 0) // KT
    follow = jnp.int32(NB - 1)
    for i in range(NB - 1, -1, -1):
        next_ref[i] = follow
        follow = jnp.where(i * SPAN + j * BLK - NEAR > lo_ref[i], i, follow)
    m_ref[...] = jnp.full(m_ref.shape, NEG, jnp.float32)
    a_ref[...] = jnp.zeros(a_ref.shape, jnp.float32)
    p1[...] = jnp.zeros(p1.shape, bf)
    f1[...] = jnp.ones(f1.shape, jnp.float32)

    def queries(b):
        marks = qa[b]
        return jnp.concatenate(
            [jnp.concatenate([q_ref[b, :, h * 128 : (h + 1) * 128], marks], 1) for h in range(4)], 0
        )

    def product(k, q):
        return lax.dot_general(k, q, (((1,), (1,)), ((), ())), preferred_element_type=jnp.float32)

    def with_ones(vt):
        return jnp.concatenate([vt, jnp.ones((16, vt.shape[1]), bf)], 0)

    for cp in copies:
        cp.wait()
    kf, af, vf = (r.reshape((NB + 1) * 8, BLK, HEAD_DIM) for r in (kb, ka, vb))
    steps = KT // BLK

    def after(b, top):
        low = top - KT
        done = low <= lo_ref[b]
        b_new = jnp.where(done, next_ref[b], b)
        over = (done & (b_new <= b)) | (top <= 0)
        return b_new, jnp.where(over, 0, jnp.where(done, b_new * SPAN + j * BLK - NEAR, low))

    def window(top):
        return (jnp.maximum(top, 0) - KT + SPAN) // BLK

    def score(b, top, s_ref, x_ref):
        at = pl.ds(window(top), steps)
        k = jnp.concatenate([kf[at].reshape(KT, HEAD_DIM), af[at].reshape(KT, BLK)], 1)
        s = product(k, queries(b))
        s_ref[...] = s
        x_ref[...] = jnp.max(s, axis=0, keepdims=True)

    def weigh(b, s_ref, x_ref, p_ref, f_ref):
        old = m_ref[b]
        new = jnp.maximum(old, x_ref[...])
        p_ref[...] = jnp.exp2((s_ref[...] - new) * SCALE2).astype(bf)
        f_ref[...] = jnp.exp2((old - new) * SCALE2)
        m_ref[b] = new

    def mix(b, top, p_ref, f_ref):
        at = window(top)
        vt = jnp.concatenate([vf[at + t] for t in range(steps)], 1)
        a_ref[b] = a_ref[b] * f_ref[...] + jnp.dot(with_ones(vt), p_ref[...], preferred_element_type=jnp.float32)

    b0, top0 = follow, follow * SPAN + j * BLK - NEAR
    score(b0, top0, sb[0], xb[0])

    def body(_, carry):
        b_old, top_old, b, top = carry
        for u in range(4):
            now, other = u % 2, (u + 1) % 2
            b_new, top_new = after(b, top)
            weigh(b, sb[now], xb[now], pb[now], fb[now])
            mix(b_old, top_old, pb[other], fb[other])
            score(b_new, top_new, sb[other], xb[other])
            b_old, top_old, b, top = b, top, b_new, top_new
        return b_old, top_old, b, top

    lax.fori_loop(0, jnp.where(total > 0, (total + 4) // 4, 0), body, (b0, top0, b0, top0))

    out = [pltpu.make_async_copy(m_ref, m_hbm, store.at[0]), pltpu.make_async_copy(a_ref, a_hbm, store.at[1])]
    for cp in out:
        cp.start()
    for cp in out:
        cp.wait()


def attend(lengths, q, kv):
    f32, bf, vmem = jnp.float32, jnp.bfloat16, pltpu.VMEM
    anywhere = pl.BlockSpec(memory_space=pl.ANY)
    return pl.pallas_call(
        attend_kernel,
        out_shape=(jax.ShapeDtypeStruct((NB, 1, QW), f32), jax.ShapeDtypeStruct((NB, 144, QW), f32)),
        grid_spec=pltpu.PrefetchScalarGridSpec(
            num_scalar_prefetch=1,
            grid=(),
            in_specs=[anywhere] * 2,
            out_specs=(anywhere, anywhere),
            scratch_shapes=[
                vmem((NB, BLK, QW), bf),
                vmem((NB + 1, 8, BLK, HEAD_DIM), bf),
                vmem((NB + 1, 8, HEAD_DIM, BLK), bf),
                vmem((NB + 1, 8, BLK, BLK), bf),
                vmem((NB, BLK, BLK), bf),
                vmem((NB, 1, QW), f32),
                vmem((NB, 144, QW), f32),
                pltpu.SMEM((NB,), jnp.int32),
                pltpu.SMEM((NB,), jnp.int32),
                vmem((KT, QW), f32),
                vmem((KT, QW), f32),
                vmem((KT, QW), bf),
                vmem((KT, QW), bf),
                vmem((1, QW), f32),
                vmem((1, QW), f32),
                vmem((1, QW), f32),
                vmem((1, QW), f32),
                pltpu.SemaphoreType.DMA((3,)),
                pltpu.SemaphoreType.DMA((2,)),
            ],
        ),
        compiler_params=pltpu.CompilerParams(vmem_limit_bytes=56 * 2**20),
    )(lengths, q, kv)


def return_kernel(
    lengths, q_hbm, kv_hbm, m_hbm, a_hbm, out_ref, q_ref, k_ref, v_ref, m_ref, a_ref, o_ref, load, load_m, send, recv, own
):
    c, j = lax.axis_index("ctx"), lax.axis_index("head")
    core, z, y = lax.rem(c, 2), lax.rem(c // 2, 4), c // 8
    bf = jnp.bfloat16

    def place(t):
        q = t // 4
        return (
            lax.rem(y + 1 - q // 2, 2) * 8
            + lax.rem(z + 3 - lax.rem(t, 4), 4) * 2
            + lax.rem(core + lax.rem((q + 1) // 2, 2), 2)
        )

    def oldest(i):
        return i * 8 + (j - 7) * ((i + 15) // 16)

    def loads(t):
        i = place(t)
        keys = pl.ds(oldest(i), 8)
        return [
            pltpu.make_async_copy(q_hbm.at[i], q_ref.at[t], load.at[0, t]),
            pltpu.make_async_copy(kv_hbm.at[0, keys], k_ref.at[t], load.at[1, t]),
            pltpu.make_async_copy(kv_hbm.at[1, keys], v_ref.at[t], load.at[2, t]),
            pltpu.make_async_copy(a_hbm.at[i], a_ref.at[t], load.at[3, t]),
        ]

    states = pltpu.make_async_copy(m_hbm, m_ref, load_m)
    states.start()
    for t in range(4):
        for cp in loads(t):
            cp.start()
    barrier = pltpu.get_barrier_semaphore()
    for t in range(NB - 1):
        pl.semaphore_signal(barrier, inc=1, device_id={"ctx": place(t), "head": j}, device_id_type=MESH)
    for t in range(4, NB):
        for cp in loads(t):
            cp.start()
    pl.semaphore_wait(barrier, NB - 1)
    states.wait()
    columns = pl.ds(pl.multiple_of(kv_head(c, j) * 1024 + core * QW, QW), QW)
    lane = lax.broadcasted_iota(jnp.int32, (1, BLK), 1)
    key = lax.broadcasted_iota(jnp.int32, (SPAN, BLK), 0)

    def returned(t):
        return remote(o_ref.at[t], out_ref.at[:, columns], send.at[t], recv.at[t], {"ctx": place(t), "head": j})

    def step(g, _):
        turns = [g * UNROLL + u for u in range(UNROLL)]
        for t in turns:
            for cp in loads(t):
                cp.wait()
        scores, parts, factors = [], [], []
        for t in turns:
            i = place(t)
            q = jnp.concatenate([q_ref[t, :, h * 128 : (h + 1) * 128] for h in range(4)], 0)
            s = lax.dot_general(
                k_ref[t].reshape(SPAN, HEAD_DIM), q, (((1,), (1,)), ((), ())), preferred_element_type=jnp.float32
            )
            row = lane + (i * SPAN + j * BLK)
            start, end = jnp.zeros((1, BLK), jnp.int32), jnp.int32(0)
            for d in range(NDOCS - 1):
                end = end + lengths[d]
                start = jnp.where(row >= end, end, start)
            base = oldest(i) * BLK
            seen = (key >= start - base) & (key <= row - base)
            s = jnp.concatenate([jnp.where(seen, s[:, h * 128 : (h + 1) * 128], NEG) for h in range(4)], 1)
            old = m_ref[i]
            top = jnp.maximum(old, jnp.max(s, axis=0, keepdims=True))
            factors.append(jnp.exp2((old - top) * SCALE2))
            parts.append(jnp.exp2((s - top) * SCALE2).astype(bf))
        for u, t in enumerate(turns):
            vt = jnp.concatenate([v_ref[t, n] for n in range(8)], 1)
            vt = jnp.concatenate([vt, jnp.ones((16, SPAN), bf)], 0)
            a = a_ref[t] * factors[u] + jnp.dot(vt, parts[u], preferred_element_type=jnp.float32)
            out = a[0:128] * (1.0 / a[128:129])
            for h in range(4):
                o_ref[t, :, h * 128 : (h + 1) * 128] = out[:, h * 128 : (h + 1) * 128].T.astype(bf)

            @pl.when(t < NB - 1)
            def _():
                returned(t).start()

        return 0

    lax.fori_loop(0, NB // UNROLL, step, 0)
    mine = pltpu.make_async_copy(o_ref.at[NB - 1], out_ref.at[:, columns], own)
    mine.start()
    mine.wait()
    for t in range(NB - 1):
        returned(t).wait()


def give_back(lengths, q, kv, m, a):
    f32, bf, vmem = jnp.float32, jnp.bfloat16, pltpu.VMEM
    dma = pltpu.SemaphoreType.DMA
    anywhere = pl.BlockSpec(memory_space=pl.ANY)
    return pl.pallas_call(
        return_kernel,
        out_shape=jax.ShapeDtypeStruct((BLK, 64 * HEAD_DIM), bf),
        in_specs=[pl.BlockSpec(memory_space=pltpu.SMEM)] + [anywhere] * 4,
        out_specs=anywhere,
        scratch_shapes=[
            vmem((NB, BLK, QW), bf),
            vmem((NB, 8, BLK, HEAD_DIM), bf),
            vmem((NB, 8, HEAD_DIM, BLK), bf),
            vmem((NB, 1, QW), f32),
            vmem((NB, 144, QW), f32),
            vmem((NB, BLK, QW), bf),
            dma((4, NB)), dma, dma((NB,)), dma((NB,)), dma,
        ],
        compiler_params=pltpu.CompilerParams(
            collective_id=1, has_side_effects=True, vmem_limit_bytes=56 * 2**20
        ),
    )(lengths, q, kv, m, a)


def on_device(queries, keys, values, doc_lengths):
    q, kv = gather(queries, keys, values)
    m, a = attend(doc_lengths, q, kv)
    return give_back(doc_lengths, q, kv.reshape(2, NB * 8, BLK, HEAD_DIM), m, a)


def solution(mesh):
    rows = P(("ctx", "head"), None)
    return jax.shard_map(on_device, mesh=mesh, in_specs=(rows, rows, rows, P()), out_specs=rows, check_vma=False)
```

```python
import functools

import jax
import jax.numpy as jnp
from jax import lax
from jax.experimental import pallas as pl
from jax.experimental.pallas import tpu as pltpu
from jax.sharding import PartitionSpec as P

MESH = pl.DeviceIdType.MESH
HEAD_DIM = 128
NDOCS = 8
NB = 16
BLK = 128
SPAN = 1024
QW = 512
KT = 512
NEAR = 7 * 128
COPIES = 4
UNROLL = 1
SCALE2 = HEAD_DIM ** -0.5 * 1.4426950408889634
NEG = -1e30


def kv_head(c, j):
    return lax.rem(c // 8 + j // 4, 2) * 4 + lax.rem(c // 2, 4)


def remote(src, dst, send, recv, device):
    return pltpu.make_async_remote_copy(
        src_ref=src, dst_ref=dst, send_sem=send, recv_sem=recv, device_id=device, device_id_type=MESH
    )


def enter(peers):
    barrier = pltpu.get_barrier_semaphore()
    for peer in peers:
        pl.semaphore_signal(barrier, inc=1, device_id=peer, device_id_type=MESH)
    pl.semaphore_wait(barrier, len(peers))


def ctx_peers(c):
    core, z, y = lax.rem(c, 2), lax.rem(c // 2, 4), c // 8
    order = [(dz, dy, dc) for dy, dc in ((0, 0), (1, 1), (1, 0), (0, 1)) for dz in (2, 1, 3, 0)]
    return [
        lax.rem(y + dy, 2) * 8 + lax.rem(z + dz, 4) * 2 + lax.rem(core + dc, 2)
        for dz, dy, dc in order
        if (dz, dy, dc) != (0, 0, 0)
    ]


def gather_kernel(q_ref, k_ref, v_ref, qg_ref, kv_ref, loc, s_q, r_q, s_1, r_1, s_g, r_g, s_b, r_b, own):
    c, j = lax.axis_index("ctx"), lax.axis_index("head")
    core, x, y = lax.rem(c, 2), lax.rem(j, 4), j // 4
    sibling = {"ctx": c + 1 - 2 * core, "head": j}
    across = {"ctx": lax.rem(c + 8, 16), "head": lax.rem(j + 4, 8)}
    right = {"ctx": c, "head": y * 4 + lax.rem(x + 1, 4)}
    left = {"ctx": c, "head": y * 4 + lax.rem(x + 3, 4)}
    others = ctx_peers(c)
    peers = [{"ctx": o, "head": j} for o in others] + [across, right, left]
    barrier = pltpu.get_barrier_semaphore()
    for peer in peers:
        pl.semaphore_signal(barrier, inc=1, device_id=peer, device_id_type=MESH)
    for h in range(8):
        loc[0, h] = k_ref[:, h * 128 : (h + 1) * 128]
        loc[1, h] = v_ref[:, h * 128 : (h + 1) * 128].T
    pl.semaphore_wait(barrier, len(peers))

    ends = []
    for n, o in enumerate(others):
        cp = remote(
            loc.at[lax.rem(o, 2), kv_head(o, j)], kv_ref.at[lax.rem(o, 2), c, j],
            s_1.at[n], r_1.at[n], {"ctx": o, "head": j},
        )
        cp.start()
        ends.append(cp)
    mine = pltpu.make_async_copy(loc.at[core, kv_head(c, j)], kv_ref.at[core, c, j], own.at[0])
    mine.start()
    columns = kv_head(c, j) * 1024 + core * QW
    mine_q = pltpu.make_async_copy(q_ref.at[:, pl.ds(pl.multiple_of(columns, QW), QW)], qg_ref.at[c], own.at[1])
    mine_q.start()
    mine.wait()
    for cp in ends:
        cp.wait_recv()

    def part(dx, dy, first, size):
        place = lax.rem(y + dy, 2) * 4 + lax.rem(x + dx, 4)
        return kv_ref.at[core, pl.ds(first, size), place]

    moves, to_sibling = [], []

    def go(ref, device):
        n = len(moves)
        cp = remote(ref, ref, s_g.at[n], r_g.at[n], device)
        cp.start()
        moves.append(cp)
        return cp

    def give(ref):
        n = len(to_sibling)
        cp = remote(ref, ref, s_b.at[n], r_b.at[n], sibling)
        cp.start()
        to_sibling.append(cp)

    a_over = go(part(0, 0, 0, 8), across)
    a_right, a_left = go(part(0, 0, 0, 8), right), go(part(0, 0, 0, 8), left)
    b_right, b_left = go(part(0, 0, 8, 8), right), go(part(0, 0, 8, 8), left)
    b_over = go(part(0, 0, 8, 8), across)
    give(part(0, 0, 0, 16))
    q_ends = []
    for n, o in enumerate(others):
        columns = kv_head(o, j) * 1024 + lax.rem(o, 2) * QW
        cp = remote(
            q_ref.at[:, pl.ds(pl.multiple_of(columns, QW), QW)], qg_ref.at[c],
            s_q.at[n], r_q.at[n], {"ctx": o, "head": j},
        )
        cp.start()
        q_ends.append(cp)
    a_over.wait_recv()
    c_right, c_left = go(part(0, 1, 0, 8), right), go(part(0, 1, 0, 8), left)
    a_right.wait_recv()
    a_far_right = go(part(3, 0, 0, 4), right)
    a_left.wait_recv()
    a_far_left = go(part(1, 0, 4, 4), left)
    b_right.wait_recv()
    b_far_right = go(part(3, 0, 8, 4), right)
    b_over_3 = go(part(3, 0, 8, 8), across)
    give(part(3, 0, 0, 16))
    b_left.wait_recv()
    b_far_left = go(part(1, 0, 12, 4), left)
    b_over_1 = go(part(1, 0, 8, 8), across)
    give(part(1, 0, 0, 16))
    b_over.wait_recv()
    give(part(0, 1, 0, 16))
    c_right.wait_recv()
    c_far_right = go(part(3, 1, 0, 4), right)
    c_left.wait_recv()
    c_far_left = go(part(1, 1, 4, 4), left)
    b_far_right.wait_recv()
    b_far_left.wait_recv()
    b_over_2 = go(part(2, 0, 8, 8), across)
    a_far_right.wait_recv()
    a_far_left.wait_recv()
    give(part(2, 0, 0, 16))
    b_over_3.wait_recv()
    give(part(3, 1, 0, 16))
    b_over_1.wait_recv()
    give(part(1, 1, 0, 16))
    c_far_right.wait_recv()
    c_far_left.wait_recv()
    b_over_2.wait_recv()
    give(part(2, 1, 0, 16))
    mine_q.wait()
    for cp in q_ends:
        cp.wait()
    for cp in ends + moves:
        cp.wait_send()
    for cp in to_sibling:
        cp.wait()


def gather(q, k, v):
    dma = pltpu.SemaphoreType.DMA
    anywhere, vmem = pl.BlockSpec(memory_space=pl.ANY), pl.BlockSpec(memory_space=pltpu.VMEM)
    return pl.pallas_call(
        gather_kernel,
        out_shape=(
            jax.ShapeDtypeStruct((NB, BLK, QW), jnp.bfloat16),
            jax.ShapeDtypeStruct((2, NB, 8, BLK, HEAD_DIM), jnp.bfloat16),
        ),
        in_specs=[anywhere, vmem, vmem],
        out_specs=(anywhere, anywhere),
        scratch_shapes=[
            pltpu.VMEM((2, 8, BLK, HEAD_DIM), jnp.bfloat16),
            dma((15,)), dma((15,)), dma((15,)), dma((15,)), dma((17,)), dma((17,)), dma((8,)), dma((8,)), dma((2,)),
        ],
        compiler_params=pltpu.CompilerParams(collective_id=0, has_side_effects=True),
    )(q, k, v)


def attend_kernel(
    lengths, q_hbm, kv_ref, m_hbm, a_hbm, q_ref, kb, vb, ka, qa, m_ref, a_ref, lo_ref, next_ref,
    s0, s1, p0, p1, f0, f1, x0, x1, load, store,
):
    sb, pb, fb, xb = (s0, s1), (p0, p1), (f0, f1), (x0, x1)
    j = lax.axis_index("head")
    bf = jnp.bfloat16
    copies = [
        pltpu.make_async_copy(q_hbm, q_ref, load.at[0]),
        pltpu.make_async_copy(kv_ref.at[0], kb.at[pl.ds(1, NB)], load.at[1]),
        pltpu.make_async_copy(kv_ref.at[1], vb.at[pl.ds(1, NB)], load.at[2]),
    ]
    for cp in copies:
        cp.start()

    lane = lax.broadcasted_iota(jnp.int32, (1, BLK), 1)
    first, last, end, ends = jnp.zeros((1, BLK), jnp.int32), jnp.full((1, BLK), 1 << 30, jnp.int32), jnp.int32(0), []
    for d in range(NDOCS):
        first = jnp.where(lane == d, end, first)
        end = end + lengths[d]
        ends.append(end)
        last = jnp.where(lane == d, end, last)
    place = lax.broadcasted_iota(jnp.int32, (BLK, BLK), 0)
    kb[0] = jnp.zeros(kb.shape[1:], bf)
    vb[0] = jnp.zeros(vb.shape[1:], bf)
    ka[0] = jnp.full(ka.shape[1:], NEG, bf)

    def mark(i, _):
        for t in range(8):
            row = place + (i * SPAN + t * BLK)
            ka[i + 1, t] = jnp.where((row >= first) & (row < last), 0.0, NEG).astype(bf)
        return 0

    lax.fori_loop(0, NB, mark, 0)
    total = jnp.int32(0)
    for i in range(NB):
        p = i * SPAN + j * BLK
        row = place + p
        qa[i] = jnp.where((row >= first) & (row < last), 1.0, 0.0).astype(bf)
        low = jnp.int32(0)
        for d in range(NDOCS - 1):
            low = jnp.where(p >= ends[d], ends[d], low)
        lo_ref[i] = low
        total = total + jnp.maximum(p - NEAR - low + KT - 1, 0) // KT
    follow = jnp.int32(NB - 1)
    for i in range(NB - 1, -1, -1):
        next_ref[i] = follow
        follow = jnp.where(i * SPAN + j * BLK - NEAR > lo_ref[i], i, follow)
    m_ref[...] = jnp.full(m_ref.shape, NEG, jnp.float32)
    a_ref[...] = jnp.zeros(a_ref.shape, jnp.float32)
    p1[...] = jnp.zeros(p1.shape, bf)
    f1[...] = jnp.ones(f1.shape, jnp.float32)

    def queries(b):
        marks = qa[b]
        return jnp.concatenate(
            [jnp.concatenate([q_ref[b, :, h * 128 : (h + 1) * 128], marks], 1) for h in range(4)], 0
        )

    def product(k, q):
        return lax.dot_general(k, q, (((1,), (1,)), ((), ())), preferred_element_type=jnp.float32)

    def with_ones(vt):
        return jnp.concatenate([vt, jnp.ones((16, vt.shape[1]), bf)], 0)

    for cp in copies:
        cp.wait()
    kf, af, vf = (r.reshape((NB + 1) * 8, BLK, HEAD_DIM) for r in (kb, ka, vb))
    steps = KT // BLK

    def after(b, top):
        low = top - KT
        done = low <= lo_ref[b]
        b_new = jnp.where(done, next_ref[b], b)
        over = (done & (b_new <= b)) | (top <= 0)
        return b_new, jnp.where(over, 0, jnp.where(done, b_new * SPAN + j * BLK - NEAR, low))

    def window(top):
        return (jnp.maximum(top, 0) - KT + SPAN) // BLK

    def score(b, top, s_ref, x_ref):
        at = pl.ds(window(top), steps)
        k = jnp.concatenate([kf[at].reshape(KT, HEAD_DIM), af[at].reshape(KT, BLK)], 1)
        s = product(k, queries(b))
        s_ref[...] = s
        x_ref[...] = jnp.max(s, axis=0, keepdims=True)

    def weigh(b, s_ref, x_ref, p_ref, f_ref):
        old = m_ref[b]
        new = jnp.maximum(old, x_ref[...])
        p_ref[...] = jnp.exp2((s_ref[...] - new) * SCALE2).astype(bf)
        f_ref[...] = jnp.exp2((old - new) * SCALE2)
        m_ref[b] = new

    def mix(b, top, p_ref, f_ref):
        at = window(top)
        vt = jnp.concatenate([vf[at + t] for t in range(steps)], 1)
        a_ref[b] = a_ref[b] * f_ref[...] + jnp.dot(with_ones(vt), p_ref[...], preferred_element_type=jnp.float32)

    b0, top0 = follow, follow * SPAN + j * BLK - NEAR
    score(b0, top0, sb[0], xb[0])

    def body(_, carry):
        b_old, top_old, b, top = carry
        for u in range(4):
            now, other = u % 2, (u + 1) % 2
            b_new, top_new = after(b, top)
            weigh(b, sb[now], xb[now], pb[now], fb[now])
            mix(b_old, top_old, pb[other], fb[other])
            score(b_new, top_new, sb[other], xb[other])
            b_old, top_old, b, top = b, top, b_new, top_new
        return b_old, top_old, b, top

    lax.fori_loop(0, jnp.where(total > 0, (total + 4) // 4, 0), body, (b0, top0, b0, top0))

    out = [pltpu.make_async_copy(m_ref, m_hbm, store.at[0]), pltpu.make_async_copy(a_ref, a_hbm, store.at[1])]
    for cp in out:
        cp.start()
    for cp in out:
        cp.wait()


def attend(lengths, q, kv):
    f32, bf, vmem = jnp.float32, jnp.bfloat16, pltpu.VMEM
    anywhere = pl.BlockSpec(memory_space=pl.ANY)
    return pl.pallas_call(
        attend_kernel,
        out_shape=(jax.ShapeDtypeStruct((NB, 1, QW), f32), jax.ShapeDtypeStruct((NB, 144, QW), f32)),
        grid_spec=pltpu.PrefetchScalarGridSpec(
            num_scalar_prefetch=1,
            grid=(),
            in_specs=[anywhere] * 2,
            out_specs=(anywhere, anywhere),
            scratch_shapes=[
                vmem((NB, BLK, QW), bf),
                vmem((NB + 1, 8, BLK, HEAD_DIM), bf),
                vmem((NB + 1, 8, HEAD_DIM, BLK), bf),
                vmem((NB + 1, 8, BLK, BLK), bf),
                vmem((NB, BLK, BLK), bf),
                vmem((NB, 1, QW), f32),
                vmem((NB, 144, QW), f32),
                pltpu.SMEM((NB,), jnp.int32),
                pltpu.SMEM((NB,), jnp.int32),
                vmem((KT, QW), f32),
                vmem((KT, QW), f32),
                vmem((KT, QW), bf),
                vmem((KT, QW), bf),
                vmem((1, QW), f32),
                vmem((1, QW), f32),
                vmem((1, QW), f32),
                vmem((1, QW), f32),
                pltpu.SemaphoreType.DMA((3,)),
                pltpu.SemaphoreType.DMA((2,)),
            ],
        ),
        compiler_params=pltpu.CompilerParams(vmem_limit_bytes=56 * 2**20),
    )(lengths, q, kv)


def return_kernel(
    lengths, q_hbm, kv_hbm, m_hbm, a_hbm, out_ref, q_ref, k_ref, v_ref, m_ref, a_ref, o_ref, load, load_m, send, recv, own
):
    c, j = lax.axis_index("ctx"), lax.axis_index("head")
    core, z, y = lax.rem(c, 2), lax.rem(c // 2, 4), c // 8
    bf = jnp.bfloat16

    def place(t):
        q = t // 4
        return (
            lax.rem(y + 1 - q // 2, 2) * 8
            + lax.rem(z + 2 + lax.rem(t, 4) // 2 * 3 + lax.rem(t, 2) * (1 + 2 * (lax.rem(t, 4) // 2)), 4) * 2
            + lax.rem(core + lax.rem((q + 1) // 2, 2), 2)
        )

    def oldest(i):
        return i * 8 + (j - 7) * ((i + 15) // 16)

    def loads(t):
        i = place(t)
        keys = pl.ds(oldest(i), 8)
        return [
            pltpu.make_async_copy(q_hbm.at[i], q_ref.at[t], load.at[0, t]),
            pltpu.make_async_copy(kv_hbm.at[0, keys], k_ref.at[t], load.at[1, t]),
            pltpu.make_async_copy(kv_hbm.at[1, keys], v_ref.at[t], load.at[2, t]),
            pltpu.make_async_copy(a_hbm.at[i], a_ref.at[t], load.at[3, t]),
        ]

    states = pltpu.make_async_copy(m_hbm, m_ref, load_m)
    states.start()
    for t in range(4):
        for cp in loads(t):
            cp.start()
    barrier = pltpu.get_barrier_semaphore()
    for t in range(NB - 1):
        pl.semaphore_signal(barrier, inc=1, device_id={"ctx": place(t), "head": j}, device_id_type=MESH)
    for t in range(4, NB):
        for cp in loads(t):
            cp.start()
    pl.semaphore_wait(barrier, NB - 1)
    states.wait()
    columns = pl.ds(pl.multiple_of(kv_head(c, j) * 1024 + core * QW, QW), QW)
    lane = lax.broadcasted_iota(jnp.int32, (1, BLK), 1)
    key = lax.broadcasted_iota(jnp.int32, (SPAN, BLK), 0)

    def returned(t):
        return remote(o_ref.at[t], out_ref.at[:, columns], send.at[t], recv.at[t], {"ctx": place(t), "head": j})

    def step(g, _):
        turns = [g * UNROLL + u for u in range(UNROLL)]
        for t in turns:
            for cp in loads(t):
                cp.wait()
        scores, parts, factors = [], [], []
        for t in turns:
            i = place(t)
            q = jnp.concatenate([q_ref[t, :, h * 128 : (h + 1) * 128] for h in range(4)], 0)
            s = lax.dot_general(
                k_ref[t].reshape(SPAN, HEAD_DIM), q, (((1,), (1,)), ((), ())), preferred_element_type=jnp.float32
            )
            row = lane + (i * SPAN + j * BLK)
            start, end = jnp.zeros((1, BLK), jnp.int32), jnp.int32(0)
            for d in range(NDOCS - 1):
                end = end + lengths[d]
                start = jnp.where(row >= end, end, start)
            base = oldest(i) * BLK
            seen = (key >= start - base) & (key <= row - base)
            s = jnp.concatenate([jnp.where(seen, s[:, h * 128 : (h + 1) * 128], NEG) for h in range(4)], 1)
            old = m_ref[i]
            top = jnp.maximum(old, jnp.max(s, axis=0, keepdims=True))
            factors.append(jnp.exp2((old - top) * SCALE2))
            parts.append(jnp.exp2((s - top) * SCALE2).astype(bf))
        for u, t in enumerate(turns):
            vt = jnp.concatenate([v_ref[t, n] for n in range(8)], 1)
            vt = jnp.concatenate([vt, jnp.ones((16, SPAN), bf)], 0)
            a = a_ref[t] * factors[u] + jnp.dot(vt, parts[u], preferred_element_type=jnp.float32)
            out = a[0:128] * (1.0 / a[128:129])
            for h in range(4):
                o_ref[t, :, h * 128 : (h + 1) * 128] = out[:, h * 128 : (h + 1) * 128].T.astype(bf)

            @pl.when(t < NB - 1)
            def _():
                returned(t).start()

        return 0

    lax.fori_loop(0, NB // UNROLL, step, 0)
    mine = pltpu.make_async_copy(o_ref.at[NB - 1], out_ref.at[:, columns], own)
    mine.start()
    mine.wait()
    for t in range(NB - 1):
        returned(t).wait()


def give_back(lengths, q, kv, m, a):
    f32, bf, vmem = jnp.float32, jnp.bfloat16, pltpu.VMEM
    dma = pltpu.SemaphoreType.DMA
    anywhere = pl.BlockSpec(memory_space=pl.ANY)
    return pl.pallas_call(
        return_kernel,
        out_shape=jax.ShapeDtypeStruct((BLK, 64 * HEAD_DIM), bf),
        in_specs=[pl.BlockSpec(memory_space=pltpu.SMEM)] + [anywhere] * 4,
        out_specs=anywhere,
        scratch_shapes=[
            vmem((NB, BLK, QW), bf),
            vmem((NB, 8, BLK, HEAD_DIM), bf),
            vmem((NB, 8, HEAD_DIM, BLK), bf),
            vmem((NB, 1, QW), f32),
            vmem((NB, 144, QW), f32),
            vmem((NB, BLK, QW), bf),
            dma((4, NB)), dma, dma((NB,)), dma((NB,)), dma,
        ],
        compiler_params=pltpu.CompilerParams(
            collective_id=1, has_side_effects=True, vmem_limit_bytes=56 * 2**20
        ),
    )(lengths, q, kv, m, a)


def copy_kernel(src, dst, held, read, write):
    rows = BLK // COPIES
    parts = [pl.ds(n * rows, rows) for n in range(COPIES)]
    reads = [pltpu.make_async_copy(src.at[p], held.at[p], read.at[n]) for n, p in enumerate(parts)]
    writes = [pltpu.make_async_copy(held.at[p], dst.at[p], write.at[n]) for n, p in enumerate(parts)]
    for cp in reads:
        cp.start()
    for a, b in zip(reads, writes):
        a.wait()
        b.start()
    for cp in writes:
        cp.wait()


def settle(x):
    anywhere = pl.BlockSpec(memory_space=pl.ANY)
    dma = pltpu.SemaphoreType.DMA
    return pl.pallas_call(
        copy_kernel,
        out_shape=jax.ShapeDtypeStruct(x.shape, x.dtype),
        in_specs=[anywhere],
        out_specs=anywhere,
        scratch_shapes=[pltpu.VMEM(x.shape, x.dtype), dma((COPIES,)), dma((COPIES,))],
        compiler_params=pltpu.CompilerParams(vmem_limit_bytes=56 * 2**20),
    )(x)


def on_device(queries, keys, values, doc_lengths):
    q, kv = gather(queries, keys, values)
    m, a = attend(doc_lengths, q, kv)
    return settle(give_back(doc_lengths, q, kv.reshape(2, NB * 8, BLK, HEAD_DIM), m, a))


def solution(mesh):
    rows = P(("ctx", "head"), None)
    return jax.shard_map(on_device, mesh=mesh, in_specs=(rows, rows, rows, P()), out_specs=rows, check_vma=False)
```
